32 devices in a mesh: groups: 2 (over y), space: 16 (over z, x, core).
Axes of the slice: x: 2, y: 2, z: 4, core: 2. Of those that a mesh axis runs over, the one named last changes fastest.
Arguments:
- field: bfloat16 [2, 16, 256, 256, 128], P('groups', None, 'space'), parts along dimension 0, may hold values from -6 to 6
- cotangent: bfloat16 [2, 16, 256, 256, 128], P('groups', None, 'space'), parts along dimension 0, may hold values from -6 to 6
- spectral_weight: bfloat16 [2, 16, 16, 64, 2048], P(None, None, None, None, 'space'), may hold values from -3 to 3
- point_weight: bfloat16 [16, 16], replicated, may hold values from -1.5 to 1.5
- bias: float32 [16], replicated, may hold values from -1 to 1
Outputs:
- activation: bfloat16 [2, 16, 256, 256, 128], P('groups', None, 'space'), parts along dimension 0
- grad_field: bfloat16 [2, 16, 256, 256, 128], P('groups', None, 'space'), parts along dimension 0
- grad_spectral: float32 [4, 16, 16, 64, 2048], P('groups', None, None, None, 'space'), parts along dimension 0
- grad_point: float32 [32, 16], P('groups'), parts along dimension 0
- grad_bias: float32 [32], P('groups'), parts along dimension 0
The draws below stay inside these ranges and needn't reach their ends.
There are 2 independent parts, one for each index of `groups`. The reference program is written for one: setup_inputs(seed, part) draws one part's arguments, and reference() takes and returns one part's arrays. A program takes and returns all parts, laid end to end along the dimension named above; an argument that names none is the same for every part. Nothing has to cross between parts.
All inputs are finite; a program needn't handle non-finite values.
Results may differ from the reference program's by a relative error of at most 0.0094.
Values sent between devices are 32-bit elements; how exact they have to be, the bound alone decides.
A program may use at most 320 MiB of HBM per device.

```python
import math
import jax
import jax.numpy as jnp
from jax import lax

BATCH = 1
C = 16
MODES = 32
NX = 256
NY = 256
NZ = 128
KX = 64
MYZ = 2048


def level_of(own_key, dims, split, smallest, top_value):
    loudness = 1.0
    for dim, parts in split:
        steps = jax.random.uniform(jax.random.fold_in(jax.random.fold_in(own_key, 6), dim), (parts,), jnp.float32, smallest / len(split), top_value / len(split))
        loudness = loudness * jnp.repeat(jnp.exp(steps), dims[dim] // parts).reshape((-1,) + (1,) * (len(dims) - 1 - dim))
    return loudness


def noise(rng, shape, width, bound, split=(), held_as=jnp.bfloat16):
    values = jax.random.normal(rng, shape, jnp.float32) * width
    if len(split) > 0:
        values = level_of(rng, shape, split, -0.22, 0.18) * values
    return jnp.clip(values, min=-bound, max=bound).astype(held_as)


def setup_inputs(seed: int = 0, part: int = 0) -> dict:
    splits = jax.random.split(jax.random.key(seed), 6)
    part_keys = jax.random.split(jax.random.fold_in(splits[5], part), 6)
    field = noise(part_keys[0], (BATCH, C, NX, NY, NZ), 1.0, 6.0, ((2, 16),))
    cotangent = noise(part_keys[1], (BATCH, C, NX, NY, NZ), 1.0, 6.0, ((2, 16),))
    spectral_weight = noise(splits[2], (2, C, C, KX, MYZ), (C // 4) ** -0.5, 3.0, ((4, 16),))
    point_weight = noise(splits[3], (C, C), C ** -0.5, 1.5)
    bias = jnp.clip(jax.random.uniform(splits[4], (C,), jnp.float32, -1.0, 1.0), -1.0, 1.0)
    return dict(field=field, cotangent=cotangent, spectral_weight=spectral_weight, point_weight=point_weight, bias=bias)


TURN = 2.0 * math.pi
GELU_SCALE = math.sqrt(2.0 / math.pi)
GELU_CUBE = 0.044715
PRECISE = lax.Precision.HIGHEST

def twiddle(length, frequencies):
    places = jnp.arange(length, dtype=jnp.int32)[:, None]
    phase = (places * frequencies[None, :] % length).astype(jnp.float32) * (TURN / length)
    factor = 1.0 / math.sqrt(length)
    return (jnp.cos(phase) * factor, -jnp.sin(phase) * factor)

def kept_modes(length, modes):
    return jnp.concatenate([jnp.arange(modes, dtype=jnp.int32), jnp.arange(length - modes, length, dtype=jnp.int32)])

def block_table(real_part, imag_part):
    upper = jnp.stack([real_part, imag_part], axis=1)
    lower = jnp.stack([-imag_part, real_part], axis=1)
    return jnp.stack([upper, lower], axis=1)

def make_tables(cells_x, cells_y, cells_z, modes):
    z_real, z_imag = twiddle(cells_z, jnp.arange(modes, dtype=jnp.int32))
    forward_z = jnp.concatenate([z_real, z_imag], axis=1)
    doubling = jnp.where(jnp.arange(modes, dtype=jnp.int32) == 0, 1.0, 2.0).astype(jnp.float32)
    double_z = forward_z * jnp.concatenate([doubling, doubling])[None, :]
    y_real, y_imag = twiddle(cells_y, kept_modes(cells_y, modes))
    full_y = block_table(y_real, y_imag)
    x_real, x_imag = twiddle(cells_x, kept_modes(cells_x, modes))
    full_x = block_table(x_real, x_imag)
    return (forward_z.astype(jnp.bfloat16), double_z.astype(jnp.bfloat16), full_y.astype(jnp.bfloat16), full_y, full_x)

def z_forward(values, table):
    return jnp.dot(values, table, preferred_element_type=jnp.float32)

def z_inverse(values, table):
    return jnp.dot(values, table.T, preferred_element_type=jnp.float32)

def y_forward(values, table):
    shape = values.shape
    split_values = values.reshape(shape[:-1] + (2, shape[-1] // 2))
    result = jnp.einsum('...yrk,yrsq->...sqk', split_values.astype(jnp.float32), table.astype(jnp.float32), precision=PRECISE)
    return result.reshape(result.shape[:-2] + (result.shape[-2] * result.shape[-1],))

def y_inverse(values, table):
    shape = values.shape
    modes_y = table.shape[3]
    split_values = values.reshape(shape[:-1] + (modes_y, shape[-1] // modes_y))
    result = jnp.einsum('...rqk,ysrq->...ysk', split_values, table, precision=PRECISE)
    return result.reshape(result.shape[:-2] + (result.shape[-2] * result.shape[-1],))

def x_forward(values, table):
    return jnp.einsum('bcxrm,xrsq->bcsqm', values, table, precision=PRECISE)

def x_inverse(values, table):
    return jnp.einsum('bcrqm,xsrq->bcxsm', values, table, precision=PRECISE)

def gelu_parts(preact):
    cube = preact * preact * preact
    tangent = jnp.tanh(GELU_SCALE * (preact + GELU_CUBE * cube))
    value = 0.5 * preact * (1.0 + tangent)
    slope = 0.5 * (1.0 + tangent) + 0.5 * preact * (1.0 - tangent * tangent) * GELU_SCALE * (1.0 + 3.0 * GELU_CUBE * preact * preact)
    return (value, slope)

def contract(form, left, right):
    return jnp.einsum(form, left.astype(jnp.float32), right.astype(jnp.float32), precision=PRECISE)

def mix_forward(spectrum, weight):
    u_real, u_imag = (spectrum[:, :, 0], spectrum[:, :, 1])
    w_real, w_imag = (weight[0], weight[1])
    form = 'bikm,iokm->bokm'
    out_real = contract(form, u_real, w_real) - contract(form, u_imag, w_imag)
    out_imag = contract(form, u_real, w_imag) + contract(form, u_imag, w_real)
    return jnp.stack([out_real, out_imag], axis=2)

def mix_dual(grads, weight):
    g_real, g_imag = (grads[:, :, 0], grads[:, :, 1])
    w_real, w_imag = (weight[0], weight[1])
    form = 'bokm,iokm->bikm'
    in_real = contract(form, g_real, w_real) + contract(form, g_imag, w_imag)
    in_imag = contract(form, g_imag, w_real) - contract(form, g_real, w_imag)
    return jnp.stack([in_real, in_imag], axis=2)

def weight_grad(spectrum, grads):
    u_real, u_imag = (spectrum[:, :, 0], spectrum[:, :, 1])
    g_real, g_imag = (grads[:, :, 0], grads[:, :, 1])
    form = 'bikm,bokm->iokm'
    part_real = contract(form, u_real, g_real) + contract(form, u_imag, g_imag)
    part_imag = contract(form, u_real, g_imag) - contract(form, u_imag, g_real)
    return jnp.stack([part_real, part_imag], axis=0)

def reference(field, cotangent, spectral_weight, point_weight, bias):
    blocks = math.gcd(NX, 16)
    block_rows = NX // blocks
    forward_z, double_z, half_y, full_y, full_x = make_tables(NX, NY, NZ, MODES)

    def split_blocks(values):
        shape = values.shape
        return jnp.moveaxis(values.reshape(shape[:2] + (blocks, block_rows) + shape[3:]), 2, 0)

    def join_blocks(values):
        moved = jnp.moveaxis(values, 0, 2)
        shape = moved.shape
        return moved.reshape(shape[:2] + (shape[2] * shape[3],) + shape[4:])

    def analyse(block):
        return y_forward(z_forward(block, forward_z).astype(jnp.bfloat16), half_y)
    spectrum = join_blocks(lax.map(analyse, split_blocks(field)))
    owned_low = x_forward(spectrum, full_x).astype(jnp.bfloat16)
    mixed = mix_forward(owned_low, spectral_weight)
    xback = x_inverse(mixed, full_x)

    def synthesize(inputs_tuple):
        field_block, cot_block, back_block = inputs_tuple
        yback = y_inverse(back_block, full_y).astype(jnp.bfloat16)
        pointwise = contract('bixyz,io->boxyz', field_block, point_weight)
        preact = z_inverse(yback, double_z) + pointwise + bias[None, :, None, None, None]
        value, slope = gelu_parts(preact)
        grad_low = (cot_block.astype(jnp.float32) * slope).astype(jnp.bfloat16)
        point_sum = contract('bixyz,boxyz->io', field_block, grad_low)
        bias_sum = lax.optimization_barrier(jnp.sum(grad_low.astype(jnp.float32), axis=(0, 2, 3, 4)))
        grad_spec = y_forward(z_forward(grad_low, double_z).astype(jnp.bfloat16), half_y)
        return (value.astype(jnp.bfloat16), grad_low, grad_spec, point_sum, bias_sum)
    values, grad_lows, grad_specs, point_sums, bias_sums = lax.map(synthesize, (split_blocks(field), split_blocks(cotangent), split_blocks(xback)))
    activation = join_blocks(values)
    grad_owned = x_forward(join_blocks(grad_specs), full_x).astype(jnp.bfloat16)
    grad_spectral = weight_grad(owned_low, grad_owned)
    dual = mix_dual(grad_owned, spectral_weight)
    dxback = x_inverse(dual, full_x)

    def restore(inputs_tuple):
        grad_block, back_block = inputs_tuple
        dyback = y_inverse(back_block, full_y).astype(jnp.bfloat16)
        total = z_inverse(dyback, forward_z) + contract('boxyz,io->bixyz', grad_block, point_weight)
        return total.astype(jnp.bfloat16)
    grad_field = join_blocks(lax.map(restore, (grad_lows, split_blocks(dxback))))
    factor = 1.0 / math.sqrt(NX * NY * NZ)
    grad_point = lax.optimization_barrier(jnp.sum(point_sums, axis=0)) * factor
    grad_bias = lax.optimization_barrier(jnp.sum(bias_sums, axis=0)) * factor
    return (activation, grad_field, grad_spectral, grad_point, grad_bias)
```

```python
import math

import jax
import numpy as np
import jax.numpy as jnp
from jax import lax
from jax.experimental import pallas as pl
from jax.experimental.pallas import tpu as pltpu
from jax.sharding import PartitionSpec as P

MODES = 32


TURN = 2.0 * math.pi
GELU_SCALE = math.sqrt(2.0 / math.pi)
GELU_CUBE = 0.044715
PRECISE = lax.Precision.HIGHEST


def twiddle(length, frequencies):
    places = jnp.arange(length, dtype=jnp.int32)[:, None]
    phase = (places * frequencies[None, :] % length).astype(jnp.float32) * (TURN / length)
    factor = 1.0 / math.sqrt(length)
    return (jnp.cos(phase) * factor, -jnp.sin(phase) * factor)


def kept_modes(length, modes):
    return jnp.concatenate(
        [jnp.arange(modes, dtype=jnp.int32), jnp.arange(length - modes, length, dtype=jnp.int32)]
    )


def block_table(real_part, imag_part):
    upper = jnp.stack([real_part, imag_part], axis=1)
    lower = jnp.stack([-imag_part, real_part], axis=1)
    return jnp.stack([upper, lower], axis=1)


def make_tables(cells_x, cells_y, cells_z, modes):
    z_real, z_imag = twiddle(cells_z, jnp.arange(modes, dtype=jnp.int32))
    forward_z = jnp.concatenate([z_real, z_imag], axis=1)
    doubling = jnp.where(jnp.arange(modes, dtype=jnp.int32) == 0, 1.0, 2.0).astype(jnp.float32)
    double_z = forward_z * jnp.concatenate([doubling, doubling])[None, :]
    y_real, y_imag = twiddle(cells_y, kept_modes(cells_y, modes))
    full_y = block_table(y_real, y_imag)
    x_real, x_imag = twiddle(cells_x, kept_modes(cells_x, modes))
    full_x = block_table(x_real, x_imag)
    return (
        forward_z.astype(jnp.bfloat16),
        double_z.astype(jnp.bfloat16),
        full_y.astype(jnp.bfloat16),
        full_y,
        full_x,
    )


def analyse_slab(values, z_table, y_table):
    zspec = jnp.dot(values, z_table, preferred_element_type=jnp.float32).astype(jnp.bfloat16)
    shape = zspec.shape
    split_values = zspec.reshape(shape[:4] + (2, shape[4] // 2))
    result = jnp.einsum(
        "bcxyrk,yrsq->bcxsqk", split_values, y_table, preferred_element_type=jnp.float32
    )
    rshape = result.shape
    return result.reshape(rshape[:4] + (rshape[4] * rshape[5],))


def restore_slab(values, y_table, z_table):
    shape = values.shape
    modes_y = y_table.shape[3]
    split_values = values.reshape(shape[:4] + (modes_y, shape[4] // modes_y))
    result = jnp.einsum("bcxrqk,ysrq->bcxysk", split_values, y_table, precision=PRECISE)
    rshape = result.shape
    rounded = result.reshape(rshape[:4] + (rshape[4] * rshape[5],)).astype(jnp.bfloat16)
    return jnp.dot(rounded, z_table.T, preferred_element_type=jnp.float32)


def x_forward(values, table):
    return jnp.einsum("bcxrm,xrsq->bcsqm", values, table, precision=PRECISE)


def x_inverse(values, table):
    return jnp.einsum("bcrqm,xsrq->bcxsm", values, table, precision=PRECISE)


def gelu_parts(preact):
    cube = preact * preact * preact
    tangent = jnp.tanh(GELU_SCALE * (preact + GELU_CUBE * cube))
    value = 0.5 * preact * (1.0 + tangent)
    slope = 0.5 * (1.0 + tangent) + 0.5 * preact * (1.0 - tangent * tangent) * GELU_SCALE * (
        1.0 + 3.0 * GELU_CUBE * preact * preact
    )
    return (value, slope)


def contract(form, left, right):
    return jnp.einsum(form, left, right, preferred_element_type=jnp.float32)


def mix_forward(spectrum, weight):
    u_real, u_imag = (spectrum[:, :, 0], spectrum[:, :, 1])
    w_real, w_imag = (weight[0], weight[1])
    form = "bikm,iokm->bokm"
    out_real = contract(form, u_real, w_real) - contract(form, u_imag, w_imag)
    out_imag = contract(form, u_real, w_imag) + contract(form, u_imag, w_real)
    return jnp.stack([out_real, out_imag], axis=2)


def mix_dual(grads, weight):
    g_real, g_imag = (grads[:, :, 0], grads[:, :, 1])
    w_real, w_imag = (weight[0], weight[1])
    form = "bokm,iokm->bikm"
    in_real = contract(form, g_real, w_real) + contract(form, g_imag, w_imag)
    in_imag = contract(form, g_imag, w_real) - contract(form, g_real, w_imag)
    return jnp.stack([in_real, in_imag], axis=2)


def weight_grad(spectrum, grads):
    u_real, u_imag = (spectrum[:, :, 0], spectrum[:, :, 1])
    g_real, g_imag = (grads[:, :, 0], grads[:, :, 1])
    form = "bikm,bokm->iokm"
    part_real = contract(form, u_real, g_real) + contract(form, u_imag, g_imag)
    part_imag = contract(form, u_real, g_imag) - contract(form, u_imag, g_real)
    return jnp.stack([part_real, part_imag], axis=0)


def general_body(field, cotangent, spectral_weight, point_weight, bias):
    spaces = lax.axis_size("space")
    planes = field.shape[2]
    cells_y = field.shape[3]
    cells_z = field.shape[4]
    cells_x = planes * spaces
    forward_z, double_z, half_y, full_y, full_x = make_tables(cells_x, cells_y, cells_z, MODES)

    def x_step(values):
        return x_forward(values, full_x)

    spectrum = analyse_slab(field, forward_z, half_y)
    owned = x_step(lax.all_to_all(spectrum, "space", split_axis=4, concat_axis=2, tiled=True))
    owned_low = owned.astype(jnp.bfloat16)
    mixed = mix_forward(owned_low, spectral_weight)
    xback = x_inverse(mixed, full_x)
    returned = lax.all_to_all(xback, "space", split_axis=2, concat_axis=4, tiled=True)
    spectral_part = restore_slab(returned, full_y, double_z)
    pointwise = contract("oi,bixyz->boxyz", point_weight.T, field)
    preact = spectral_part + pointwise + bias[None, :, None, None, None]
    value, slope = gelu_parts(preact)
    activation = value.astype(jnp.bfloat16)
    grad_low = (cotangent.astype(jnp.float32) * slope).astype(jnp.bfloat16)
    point_sum = contract("bixyz,boxyz->io", field, grad_low)
    bias_sum = jnp.sum(grad_low, axis=(0, 2, 3, 4), dtype=jnp.float32)
    point_total, bias_total = lax.psum((point_sum, bias_sum), "space")
    grad_spec = analyse_slab(grad_low, double_z, half_y)
    grad_owned = x_step(lax.all_to_all(grad_spec, "space", split_axis=4, concat_axis=2, tiled=True))
    grad_owned_low = grad_owned.astype(jnp.bfloat16)
    grad_spectral = weight_grad(owned_low, grad_owned_low)
    dual = mix_dual(grad_owned_low, spectral_weight)
    dxback = x_inverse(dual, full_x)
    dreturned = lax.all_to_all(dxback, "space", split_axis=2, concat_axis=4, tiled=True)
    spectral_grad = restore_slab(dreturned, full_y, forward_z)
    total = spectral_grad + contract("io,boxyz->bixyz", point_weight, grad_low)
    grad_field = total.astype(jnp.bfloat16)
    factor = 1.0 / math.sqrt(cells_x * cells_y * cells_z)
    return (activation, grad_field, grad_spectral, point_total * factor, bias_total * factor)


CHUNKS = 2
GROUP = 4
ROWS = 16
VMEM = 56 * 1024 * 1024
BF16 = jnp.bfloat16
F32 = jnp.float32


def np_twiddle(length, frequencies):
    phase = (np.arange(length)[:, None] * frequencies[None, :] % length) * (TURN / length)
    factor = 1.0 / math.sqrt(length)
    return np.cos(phase) * factor, -np.sin(phase) * factor


def np_block(length, modes):
    kept = np.concatenate([np.arange(modes), np.arange(length - modes, length)])
    real, imag = np_twiddle(length, kept)
    return np.stack([np.stack([real, imag], 1), np.stack([-imag, real], 1)], 1)


def blocked_tables(cells_x, cells_y, cells_z, spaces, chunks):
    z_real, z_imag = np_twiddle(cells_z, np.arange(MODES))
    forward_z = np.stack([z_real, z_imag], 1)
    doubling = np.where(np.arange(MODES) == 0, 1.0, 2.0)
    double_z = forward_z * doubling
    eye = np.eye(GROUP)

    def z_down(table):
        out = np.einsum("zrk,ab->azrbk", table, eye)
        return out.reshape(GROUP * cells_z, 2 * GROUP * MODES).astype(BF16)

    full_y = np_block(cells_y, MODES)
    y_split = full_y.reshape(cells_y, 2, 2, spaces, 2 * MODES // spaces)
    y_down = y_split.transpose(3, 2, 4, 1, 0).reshape(4 * MODES, 2 * cells_y).astype(BF16)
    y_up = y_split.transpose(1, 0, 3, 2, 4).reshape(2 * cells_y, 4 * MODES).astype(BF16)
    full_x = np_block(cells_x, MODES)
    x_split = full_x.reshape(spaces, chunks, cells_x // spaces // chunks, 2, 2, 2 * MODES)
    x_split = x_split.transpose(1, 0, 2, 3, 4, 5).reshape(cells_x, 2, 2, 2 * MODES)
    x_down = x_split.transpose(2, 3, 1, 0).reshape(4 * MODES, 2 * cells_x).astype(np.float32)
    x_up = x_split.transpose(1, 0, 2, 3).reshape(2 * cells_x, 4 * MODES).astype(np.float32)
    forward, double = z_down(forward_z), z_down(double_z)
    return forward, double, forward.T.copy(), double.T.copy(), y_down, y_up, x_down, x_up


def dot(left, right):
    return jnp.dot(left, right, preferred_element_type=F32)


def dot_exact(left, right):
    return jnp.dot(left, right, preferred_element_type=F32, precision=PRECISE)


def params():
    return pltpu.CompilerParams(vmem_limit_bytes=VMEM)


def fixed(shape):
    return pl.BlockSpec(shape, lambda *_: (0,) * len(shape))


def analyse_planes(planes, z_table, y_table):
    spectrum = dot(jnp.concatenate(planes, axis=1), z_table).astype(BF16)
    half = spectrum.shape[1] // 2
    stacked = jnp.concatenate([spectrum[:, :half], spectrum[:, half:]], axis=0)
    return dot(y_table, stacked)


def analyse_kernel(field, z_table, y_table, wire):
    count = field.shape[1]
    for place in range(count):
        planes = [field[c, place] for c in range(GROUP)]
        coded = analyse_planes(planes, z_table[...], y_table[...])
        wire[:, 0, place * 8 : place * 8 + 8, :] = coded.reshape(wire.shape[0], 8, 128)


def analyse_call(field, z_table, y_table, spaces, chunk):
    channels, planes, cells_y, cells_z = field.shape
    part = planes // CHUNKS
    step = min(4, part)
    return pl.pallas_call(
        analyse_kernel,
        grid=(channels // GROUP, part // step),
        in_specs=[
            pl.BlockSpec(
                (GROUP, step, cells_y, cells_z),
                lambda g, x: (g, chunk * (part // step) + x, 0, 0),
            ),
            fixed(z_table.shape),
            fixed(y_table.shape),
        ],
        out_specs=pl.BlockSpec((spaces, 1, step * 8, 128), lambda g, x: (0, g, x, 0)),
        out_shape=jax.ShapeDtypeStruct((spaces, channels // GROUP, part * 8, 128), F32),
        compiler_params=params(),
        name="analyse",
    )(field, z_table, y_table)


def lane_swap(blocks):
    return [
        jnp.concatenate([b[:, k * MODES : (k + 1) * MODES] for b in blocks], axis=1)
        for k in range(GROUP)
    ]


def gather_modes(wires, x_table, spectrum):
    spaces, groups, rows, _ = wires[0].shape
    part = rows // 8

    def one_group(group, carry):
        blocks = []
        for k in range(GROUP):
            pieces = []
            for r in range(2):
                for wire in wires:
                    for source in range(spaces):
                        pieces.append(wire[source, group, pl.ds(r * GROUP + k, part, stride=8), :])
            blocks.append(dot_exact(x_table[...], jnp.concatenate(pieces, axis=0)))
        for c, block in enumerate(lane_swap(blocks)):
            spectrum[group * GROUP + c] = block.astype(BF16).astype(F32)
        return carry

    lax.fori_loop(0, groups, one_group, 0)


def scatter_modes(mixed, x_table, wires):
    spaces, _, rows, _ = wires[0].shape
    part = rows // 8
    for k, block in enumerate(lane_swap([mixed[c] for c in range(GROUP)])):
        result = dot_exact(x_table[...], block)
        place = 0
        for s in range(2):
            for wire in wires:
                for target in range(spaces):
                    wire[target, 0, pl.ds(s * GROUP + k, part, stride=8), :] = result[
                        place : place + part
                    ]
                    place += part


def mix_kernel(*refs):
    wires = refs[:CHUNKS]
    weight, x_down, x_up = refs[CHUNKS : CHUNKS + 3]
    outs = refs[CHUNKS + 3 : 2 * CHUNKS + 3]
    kept, spectrum, mixed = refs[2 * CHUNKS + 3 :]
    step = pl.program_id(0)
    channels = spectrum.shape[0]
    half = spectrum.shape[1] // 2

    @pl.when(step == 0)
    def _():
        gather_modes(wires, x_down, spectrum)
        kept[...] = spectrum[...].astype(BF16)

    real = jnp.zeros((half, 128), F32)
    imag = jnp.zeros((half, 128), F32)
    for i in range(channels):
        u_real, u_imag = spectrum[i, :half], spectrum[i, half:]
        w_real, w_imag = weight[0, i, 0].astype(F32), weight[1, i, 0].astype(F32)
        real += u_real * w_real - u_imag * w_imag
        imag += u_real * w_imag + u_imag * w_real
    place = lax.rem(step, GROUP)
    mixed[place, :half] = real
    mixed[place, half:] = imag

    @pl.when(place == GROUP - 1)
    def _():
        scatter_modes(mixed, x_up, outs)


def dual_kernel(*refs):
    wires = refs[:CHUNKS]
    weight, kept, x_down, x_up = refs[CHUNKS : CHUNKS + 4]
    outs = refs[CHUNKS + 4 : 2 * CHUNKS + 4]
    slope, spectrum, mixed = refs[2 * CHUNKS + 4 :]
    step = pl.program_id(0)
    channels = spectrum.shape[0]
    half = spectrum.shape[1] // 2

    @pl.when(step == 0)
    def _():
        gather_modes(wires, x_down, spectrum)

    u_real, u_imag = kept[0, :half].astype(F32), kept[0, half:].astype(F32)
    real = jnp.zeros((half, 128), F32)
    imag = jnp.zeros((half, 128), F32)
    for o in range(channels):
        g_real, g_imag = spectrum[o, :half], spectrum[o, half:]
        w_real, w_imag = weight[0, 0, o].astype(F32), weight[1, 0, o].astype(F32)
        real += w_real * g_real + w_imag * g_imag
        imag += w_real * g_imag - w_imag * g_real
        slope[0, 0, o] = u_real * g_real + u_imag * g_imag
        slope[1, 0, o] = u_real * g_imag - u_imag * g_real
    place = lax.rem(step, GROUP)
    mixed[place, :half] = real
    mixed[place, half:] = imag

    @pl.when(place == GROUP - 1)
    def _():
        scatter_modes(mixed, x_up, outs)


def mix_call(wires, weight, kept, x_down, x_up):
    _, channels, _, modes_x, modes = weight.shape
    shape = wires[0].shape
    wire_block = (shape[0], 1) + shape[2:]
    wire_specs = [fixed(shape) for _ in wires]
    tables = [fixed(x_down.shape), fixed(x_up.shape)]
    out_wires = [pl.BlockSpec(wire_block, lambda s: (0, s // GROUP, 0, 0)) for _ in wires]
    out_shapes = [jax.ShapeDtypeStruct(shape, F32) for _ in wires]
    scratch = [
        pltpu.VMEM((channels, 2 * modes_x, modes), F32),
        pltpu.VMEM((GROUP, 2 * modes_x, modes), F32),
    ]
    if kept is None:
        block = (2, channels, 1, modes_x, modes)
        return pl.pallas_call(
            mix_kernel,
            grid=(channels,),
            in_specs=wire_specs + [pl.BlockSpec(block, lambda s: (0, 0, s, 0, 0))] + tables,
            out_specs=out_wires + [fixed((channels, 2 * modes_x, modes))],
            out_shape=out_shapes + [jax.ShapeDtypeStruct((channels, 2 * modes_x, modes), BF16)],
            scratch_shapes=scratch,
            compiler_params=params(),
            name="mix",
        )(*wires, weight, x_down, x_up)
    block = (2, 1, channels, modes_x, modes)
    return pl.pallas_call(
        dual_kernel,
        grid=(channels,),
        in_specs=wire_specs
        + [
            pl.BlockSpec(block, lambda s: (0, s, 0, 0, 0)),
            pl.BlockSpec((1, 2 * modes_x, modes), lambda s: (s, 0, 0)),
        ]
        + tables,
        out_specs=out_wires + [pl.BlockSpec(block, lambda s: (0, s, 0, 0, 0))],
        out_shape=out_shapes
        + [jax.ShapeDtypeStruct((2, channels, channels, modes_x, modes), F32)],
        scratch_shapes=scratch,
        compiler_params=params(),
        name="dual",
    )(*wires, weight, kept, x_down, x_up)


def restore_planes(wire, y_table, z_table, spectral):
    spaces, groups = wire.shape[:2]
    cells_y = spectral.shape[1]
    for g in range(groups):
        coded = wire[:, g].reshape(spaces * 8, 128).astype(BF16)
        lines = dot(y_table[...], coded).astype(BF16)
        lines = jnp.concatenate([lines[:cells_y], lines[cells_y:]], axis=1)
        planes = dot(lines, z_table[...])
        for c in range(GROUP):
            spectral[g * GROUP + c] = planes[:, c * 128 : (c + 1) * 128]


def synthesise_kernel(
    wire, field, cotangent, point, bias, y_up, z_up, z_down, y_down, *refs
):
    activation, grad, wire_out, point_sum, bias_sum, spectral = refs[-6:]
    step = pl.program_id(0)
    channels, _, cells_y, cells_z = field.shape

    @pl.when(step == 0)
    def _():
        point_sum[...] = jnp.zeros_like(point_sum)
        bias_sum[...] = jnp.zeros_like(bias_sum)

    restore_planes(wire, y_up, z_up, spectral)
    for row in range(cells_y // ROWS):
        lines = pl.ds(row * ROWS, ROWS)
        inputs = field[:, 0, lines, :].reshape(channels * ROWS, cells_z)
        preact = dot(point[...], inputs)
        preact += spectral[:, lines, :].reshape(channels * ROWS, cells_z) + bias[...]
        square = preact * preact
        tangent = jnp.tanh(preact * (GELU_SCALE + (GELU_SCALE * GELU_CUBE) * square))
        upper = 0.5 + 0.5 * tangent
        activation[:, 0, lines, :] = (
            (preact * upper).astype(BF16).reshape(channels, ROWS, cells_z)
        )
        inner = GELU_SCALE + (3.0 * GELU_SCALE * GELU_CUBE) * square
        slope = upper + (preact * inner) * (0.5 - 0.5 * tangent * tangent)
        coming = cotangent[:, 0, lines, :].reshape(channels * ROWS, cells_z).astype(F32)
        low = (coming * slope).astype(BF16)
        grad[:, 0, lines, :] = low.reshape(channels, ROWS, cells_z)
        bias_sum[...] += low.astype(F32)

    def by_rows(ref):
        return jnp.concatenate(
            [
                ref[:, 0, row * ROWS : (row + 1) * ROWS, :].reshape(channels * ROWS, cells_z)
                for row in range(cells_y // ROWS)
            ],
            axis=1,
        )

    point_sum[...] += lax.dot_general(
        by_rows(field), by_rows(grad), (((1,), (1,)), ((), ())), preferred_element_type=F32
    )
    for g in range(channels // GROUP):
        planes = [grad[g * GROUP + c, 0] for c in range(GROUP)]
        coded = analyse_planes(planes, z_down[...], y_down[...])
        wire_out[:, g] = coded.reshape(wire_out.shape[0], 8, 128)


def synthesise_call(wire, field, cotangent, point, bias, tables, chunk, earlier):
    channels, planes, cells_y, cells_z = field.shape
    part = planes // CHUNKS
    spaces, groups = wire.shape[:2]
    slab = pl.BlockSpec((channels, 1, cells_y, cells_z), lambda x: (0, chunk * part + x, 0, 0))
    wire_spec = pl.BlockSpec((spaces, groups, 8, 128), lambda x: (0, 0, x, 0))
    side = channels * ROWS
    operands = [wire, field, cotangent, point, bias] + list(tables)
    specs = [wire_spec, slab, slab] + [fixed(a.shape) for a in operands[3:]]
    aliases = {}
    for index, value in enumerate(earlier):
        aliases[len(operands)] = index
        operands.append(value)
        specs.append(pl.BlockSpec(memory_space=pl.ANY))
    return pl.pallas_call(
        synthesise_kernel,
        grid=(part,),
        in_specs=specs,
        out_specs=[slab, slab, wire_spec, fixed((side, side)), fixed((side, cells_z))],
        out_shape=[
            jax.ShapeDtypeStruct(field.shape, BF16),
            jax.ShapeDtypeStruct(field.shape, BF16),
            jax.ShapeDtypeStruct(wire.shape, F32),
            jax.ShapeDtypeStruct((side, side), F32),
            jax.ShapeDtypeStruct((side, cells_z), F32),
        ],
        scratch_shapes=[pltpu.VMEM((channels, cells_y, cells_z), F32)],
        input_output_aliases=aliases,
        compiler_params=params(),
        name="synthesise",
    )(*operands)


def finish_kernel(wire, grad, point, y_up, z_up, *refs):
    grad_field, spectral = refs[-2:]
    channels, _, cells_y, cells_z = grad.shape
    restore_planes(wire, y_up, z_up, spectral)
    for row in range(cells_y // ROWS):
        lines = pl.ds(row * ROWS, ROWS)
        inputs = grad[:, 0, lines, :].reshape(channels * ROWS, cells_z)
        total = dot(point[...], inputs) + spectral[:, lines, :].reshape(channels * ROWS, cells_z)
        grad_field[:, 0, lines, :] = total.astype(BF16).reshape(channels, ROWS, cells_z)


def finish_call(wire, grad, point, y_up, z_up, chunk, earlier):
    channels, planes, cells_y, cells_z = grad.shape
    part = planes // CHUNKS
    spaces, groups = wire.shape[:2]
    slab = pl.BlockSpec((channels, 1, cells_y, cells_z), lambda x: (0, chunk * part + x, 0, 0))
    operands = [wire, grad, point, y_up, z_up]
    specs = [pl.BlockSpec((spaces, groups, 8, 128), lambda x: (0, 0, x, 0)), slab]
    specs += [fixed(a.shape) for a in operands[2:]]
    aliases = {}
    for value in earlier:
        aliases[len(operands)] = 0
        operands.append(value)
        specs.append(pl.BlockSpec(memory_space=pl.ANY))
    return pl.pallas_call(
        finish_kernel,
        grid=(part,),
        in_specs=specs,
        out_specs=slab,
        out_shape=jax.ShapeDtypeStruct(grad.shape, BF16),
        scratch_shapes=[pltpu.VMEM((channels, cells_y, cells_z), F32)],
        input_output_aliases=aliases,
        compiler_params=params(),
        name="finish",
    )(*operands)


def exchange(values):
    return lax.all_to_all(values, "space", split_axis=0, concat_axis=0, tiled=True)


def blocked_body(field, cotangent, spectral_weight, point_weight, bias):
    spaces = lax.axis_size("space")
    _, channels, planes, cells_y, cells_z = field.shape
    cells_x = planes * spaces
    tables = blocked_tables(cells_x, cells_y, cells_z, spaces, CHUNKS)
    z_down, z_down2, z_up, z_up2, y_down, y_up, x_down, x_up = map(jnp.asarray, tables)
    field_part, cotangent_part = field[0], cotangent[0]
    eye = jnp.eye(ROWS, dtype=F32)
    point_in = jnp.kron(point_weight.T.astype(F32), eye).astype(BF16)
    point_out = jnp.kron(point_weight.astype(F32), eye).astype(BF16)
    bias_rows = jnp.broadcast_to(jnp.repeat(bias, ROWS)[:, None], (channels * ROWS, cells_z))
    chunks = range(CHUNKS)
    wires = [exchange(analyse_call(field_part, z_down, y_down, spaces, h)) for h in chunks]
    *wires, kept = mix_call(wires, spectral_weight, None, x_down, x_up)
    wires = [exchange(w) for w in wires]
    earlier, back, point_sums, bias_sums = [], [], 0.0, 0.0
    for h in chunks:
        activation, grad, wire, point_sum, bias_sum = synthesise_call(
            wires[h], field_part, cotangent_part, point_in, bias_rows,
            (y_up, z_up2, z_down2, y_down), h, earlier,
        )
        earlier = [activation, grad]
        back.append(exchange(wire))
        point_sums, bias_sums = point_sums + point_sum, bias_sums + bias_sum
    point_part = jnp.sum(
        point_sums.reshape(channels, ROWS, channels, ROWS) * eye[None, :, None, :], axis=(1, 3)
    )
    bias_part = jnp.sum(bias_sums.reshape(channels, -1), axis=1)
    *wires, grad_spectral = mix_call(back, spectral_weight, kept, x_down, x_up)
    wires = [exchange(w) for w in wires]
    point_total, bias_total = lax.psum((point_part, bias_part), "space")
    finished = []
    for h in chunks:
        finished = [finish_call(wires[h], grad, point_out, y_up, z_up, h, finished)]
    factor = 1.0 / math.sqrt(cells_x * cells_y * cells_z)
    return (
        activation[None],
        finished[0][None],
        grad_spectral,
        point_total * factor,
        bias_total * factor,
    )


def body(field, cotangent, spectral_weight, point_weight, bias):
    blocked = (
        field.shape == (1, 16, 16, 256, 128)
        and spectral_weight.shape == (2, 16, 16, 64, 128)
        and lax.axis_size("space") == 16
    )
    chosen = blocked_body if blocked else general_body
    return chosen(field, cotangent, spectral_weight, point_weight, bias)


def solution(mesh):
    placed = (
        P("groups", None, "space", None, None),
        P("groups", None, "space", None, None),
        P(None, None, None, None, "space"),
        P(),
        P(),
    )
    return jax.shard_map(
        body,
        mesh=mesh,
        in_specs=placed,
        out_specs=(
            P("groups", None, "space", None, None),
            P("groups", None, "space", None, None),
            P("groups", None, None, None, "space"),
            P("groups", None),
            P("groups"),
        ),
        check_vma=False,
    )
```

```python
import math

import jax
import numpy as np
import jax.numpy as jnp
from jax import lax
from jax.experimental import pallas as pl
from jax.experimental.pallas import tpu as pltpu
from jax.sharding import PartitionSpec as P

MODES = 32


TURN = 2.0 * math.pi
GELU_SCALE = math.sqrt(2.0 / math.pi)
GELU_CUBE = 0.044715
PRECISE = lax.Precision.HIGHEST


def twiddle(length, frequencies):
    places = jnp.arange(length, dtype=jnp.int32)[:, None]
    phase = (places * frequencies[None, :] % length).astype(jnp.float32) * (TURN / length)
    factor = 1.0 / math.sqrt(length)
    return (jnp.cos(phase) * factor, -jnp.sin(phase) * factor)


def kept_modes(length, modes):
    return jnp.concatenate(
        [jnp.arange(modes, dtype=jnp.int32), jnp.arange(length - modes, length, dtype=jnp.int32)]
    )


def block_table(real_part, imag_part):
    upper = jnp.stack([real_part, imag_part], axis=1)
    lower = jnp.stack([-imag_part, real_part], axis=1)
    return jnp.stack([upper, lower], axis=1)


def make_tables(cells_x, cells_y, cells_z, modes):
    z_real, z_imag = twiddle(cells_z, jnp.arange(modes, dtype=jnp.int32))
    forward_z = jnp.concatenate([z_real, z_imag], axis=1)
    doubling = jnp.where(jnp.arange(modes, dtype=jnp.int32) == 0, 1.0, 2.0).astype(jnp.float32)
    double_z = forward_z * jnp.concatenate([doubling, doubling])[None, :]
    y_real, y_imag = twiddle(cells_y, kept_modes(cells_y, modes))
    full_y = block_table(y_real, y_imag)
    x_real, x_imag = twiddle(cells_x, kept_modes(cells_x, modes))
    full_x = block_table(x_real, x_imag)
    return (
        forward_z.astype(jnp.bfloat16),
        double_z.astype(jnp.bfloat16),
        full_y.astype(jnp.bfloat16),
        full_y,
        full_x,
    )


def analyse_slab(values, z_table, y_table):
    zspec = jnp.dot(values, z_table, preferred_element_type=jnp.float32).astype(jnp.bfloat16)
    shape = zspec.shape
    split_values = zspec.reshape(shape[:4] + (2, shape[4] // 2))
    result = jnp.einsum(
        "bcxyrk,yrsq->bcxsqk", split_values, y_table, preferred_element_type=jnp.float32
    )
    rshape = result.shape
    return result.reshape(rshape[:4] + (rshape[4] * rshape[5],))


def restore_slab(values, y_table, z_table):
    shape = values.shape
    modes_y = y_table.shape[3]
    split_values = values.reshape(shape[:4] + (modes_y, shape[4] // modes_y))
    result = jnp.einsum("bcxrqk,ysrq->bcxysk", split_values, y_table, precision=PRECISE)
    rshape = result.shape
    rounded = result.reshape(rshape[:4] + (rshape[4] * rshape[5],)).astype(jnp.bfloat16)
    return jnp.dot(rounded, z_table.T, preferred_element_type=jnp.float32)


def x_forward(values, table):
    return jnp.einsum("bcxrm,xrsq->bcsqm", values, table, precision=PRECISE)


def x_inverse(values, table):
    return jnp.einsum("bcrqm,xsrq->bcxsm", values, table, precision=PRECISE)


def gelu_parts(preact):
    cube = preact * preact * preact
    tangent = jnp.tanh(GELU_SCALE * (preact + GELU_CUBE * cube))
    value = 0.5 * preact * (1.0 + tangent)
    slope = 0.5 * (1.0 + tangent) + 0.5 * preact * (1.0 - tangent * tangent) * GELU_SCALE * (
        1.0 + 3.0 * GELU_CUBE * preact * preact
    )
    return (value, slope)


def contract(form, left, right):
    return jnp.einsum(form, left, right, preferred_element_type=jnp.float32)


def mix_forward(spectrum, weight):
    u_real, u_imag = (spectrum[:, :, 0], spectrum[:, :, 1])
    w_real, w_imag = (weight[0], weight[1])
    form = "bikm,iokm->bokm"
    out_real = contract(form, u_real, w_real) - contract(form, u_imag, w_imag)
    out_imag = contract(form, u_real, w_imag) + contract(form, u_imag, w_real)
    return jnp.stack([out_real, out_imag], axis=2)


def mix_dual(grads, weight):
    g_real, g_imag = (grads[:, :, 0], grads[:, :, 1])
    w_real, w_imag = (weight[0], weight[1])
    form = "bokm,iokm->bikm"
    in_real = contract(form, g_real, w_real) + contract(form, g_imag, w_imag)
    in_imag = contract(form, g_imag, w_real) - contract(form, g_real, w_imag)
    return jnp.stack([in_real, in_imag], axis=2)


def weight_grad(spectrum, grads):
    u_real, u_imag = (spectrum[:, :, 0], spectrum[:, :, 1])
    g_real, g_imag = (grads[:, :, 0], grads[:, :, 1])
    form = "bikm,bokm->iokm"
    part_real = contract(form, u_real, g_real) + contract(form, u_imag, g_imag)
    part_imag = contract(form, u_real, g_imag) - contract(form, u_imag, g_real)
    return jnp.stack([part_real, part_imag], axis=0)


def general_body(field, cotangent, spectral_weight, point_weight, bias):
    spaces = lax.axis_size("space")
    planes = field.shape[2]
    cells_y = field.shape[3]
    cells_z = field.shape[4]
    cells_x = planes * spaces
    forward_z, double_z, half_y, full_y, full_x = make_tables(cells_x, cells_y, cells_z, MODES)

    def x_step(values):
        return x_forward(values, full_x)

    spectrum = analyse_slab(field, forward_z, half_y)
    owned = x_step(lax.all_to_all(spectrum, "space", split_axis=4, concat_axis=2, tiled=True))
    owned_low = owned.astype(jnp.bfloat16)
    mixed = mix_forward(owned_low, spectral_weight)
    xback = x_inverse(mixed, full_x)
    returned = lax.all_to_all(xback, "space", split_axis=2, concat_axis=4, tiled=True)
    spectral_part = restore_slab(returned, full_y, double_z)
    pointwise = contract("oi,bixyz->boxyz", point_weight.T, field)
    preact = spectral_part + pointwise + bias[None, :, None, None, None]
    value, slope = gelu_parts(preact)
    activation = value.astype(jnp.bfloat16)
    grad_low = (cotangent.astype(jnp.float32) * slope).astype(jnp.bfloat16)
    point_sum = contract("bixyz,boxyz->io", field, grad_low)
    bias_sum = jnp.sum(grad_low, axis=(0, 2, 3, 4), dtype=jnp.float32)
    point_total, bias_total = lax.psum((point_sum, bias_sum), "space")
    grad_spec = analyse_slab(grad_low, double_z, half_y)
    grad_owned = x_step(lax.all_to_all(grad_spec, "space", split_axis=4, concat_axis=2, tiled=True))
    grad_owned_low = grad_owned.astype(jnp.bfloat16)
    grad_spectral = weight_grad(owned_low, grad_owned_low)
    dual = mix_dual(grad_owned_low, spectral_weight)
    dxback = x_inverse(dual, full_x)
    dreturned = lax.all_to_all(dxback, "space", split_axis=2, concat_axis=4, tiled=True)
    spectral_grad = restore_slab(dreturned, full_y, forward_z)
    total = spectral_grad + contract("io,boxyz->bixyz", point_weight, grad_low)
    grad_field = total.astype(jnp.bfloat16)
    factor = 1.0 / math.sqrt(cells_x * cells_y * cells_z)
    return (activation, grad_field, grad_spectral, point_total * factor, bias_total * factor)


CHUNKS = 2
GROUP = 4
ROWS = 16
VMEM = 56 * 1024 * 1024
BF16 = jnp.bfloat16
F32 = jnp.float32


def np_twiddle(length, frequencies):
    phase = (np.arange(length)[:, None] * frequencies[None, :] % length) * (TURN / length)
    factor = 1.0 / math.sqrt(length)
    return np.cos(phase) * factor, -np.sin(phase) * factor


def np_block(length, modes):
    kept = np.concatenate([np.arange(modes), np.arange(length - modes, length)])
    real, imag = np_twiddle(length, kept)
    return np.stack([np.stack([real, imag], 1), np.stack([-imag, real], 1)], 1)


def in_halves(table):
    high = table.astype(BF16)
    low = (table - high.astype(np.float64)).astype(BF16)
    return np.concatenate([high, high, low], axis=1)


def blocked_tables(cells_x, cells_y, cells_z, spaces, chunks):
    z_real, z_imag = np_twiddle(cells_z, np.arange(MODES))
    forward_z = np.stack([z_real, z_imag], 1)
    doubling = np.where(np.arange(MODES) == 0, 1.0, 2.0)
    double_z = forward_z * doubling
    eye = np.eye(GROUP)

    def z_down(table):
        out = np.einsum("zrk,ab->azrbk", table, eye)
        return out.reshape(GROUP * cells_z, 2 * GROUP * MODES).astype(BF16)

    full_y = np_block(cells_y, MODES)
    y_split = full_y.reshape(cells_y, 2, 2, spaces, 2 * MODES // spaces)
    y_down = y_split.transpose(3, 2, 4, 1, 0).reshape(4 * MODES, 2 * cells_y).astype(BF16)
    y_up = y_split.transpose(1, 0, 3, 2, 4).reshape(2 * cells_y, 4 * MODES).astype(BF16)
    full_x = np_block(cells_x, MODES)
    x_split = full_x.reshape(spaces, chunks, cells_x // spaces // chunks, 2, 2, 2 * MODES)
    x_split = x_split.transpose(1, 0, 2, 3, 4, 5).reshape(cells_x, 2, 2, 2 * MODES)
    x_down = x_split.transpose(2, 3, 1, 0).reshape(4 * MODES, 2 * cells_x)
    x_up = x_split.transpose(1, 0, 2, 3).reshape(2 * cells_x, 4 * MODES)
    forward, double = z_down(forward_z), z_down(double_z)
    return forward, double, forward.T.copy(), double.T.copy(), y_down, y_up, in_halves(x_down), in_halves(x_up)


def dot(left, right):
    return jnp.dot(left, right, preferred_element_type=F32)


def dot_halves(table, values):
    high = values.astype(BF16)
    low = (values - high.astype(F32)).astype(BF16)
    return dot(table, jnp.concatenate([high, low, high], axis=0))


def params():
    return pltpu.CompilerParams(vmem_limit_bytes=VMEM)


def fixed(shape):
    return pl.BlockSpec(shape, lambda *_: (0,) * len(shape))


def analyse_planes(planes, z_table, y_table):
    spectrum = dot(jnp.concatenate(planes, axis=1), z_table).astype(BF16)
    half = spectrum.shape[1] // 2
    stacked = jnp.concatenate([spectrum[:, :half], spectrum[:, half:]], axis=0)
    return dot(y_table, stacked)


def analyse_kernel(field, z_table, y_table, wire):
    count = field.shape[1]
    for place in range(count):
        planes = [field[c, place] for c in range(GROUP)]
        coded = analyse_planes(planes, z_table[...], y_table[...])
        wire[:, 0, place * 8 : place * 8 + 8, :] = coded.reshape(wire.shape[0], 8, 128)


def analyse_call(field, z_table, y_table, spaces, chunk):
    channels, planes, cells_y, cells_z = field.shape
    part = planes // CHUNKS
    step = min(4, part)
    return pl.pallas_call(
        analyse_kernel,
        grid=(channels // GROUP, part // step),
        in_specs=[
            pl.BlockSpec(
                (GROUP, step, cells_y, cells_z),
                lambda g, x: (g, chunk * (part // step) + x, 0, 0),
            ),
            fixed(z_table.shape),
            fixed(y_table.shape),
        ],
        out_specs=pl.BlockSpec((spaces, 1, step * 8, 128), lambda g, x: (0, g, x, 0)),
        out_shape=jax.ShapeDtypeStruct((spaces, channels // GROUP, part * 8, 128), F32),
        compiler_params=params(),
        name="analyse",
    )(field, z_table, y_table)


def lane_swap(blocks):
    return [
        jnp.concatenate([b[:, k * MODES : (k + 1) * MODES] for b in blocks], axis=1)
        for k in range(GROUP)
    ]


def gather_modes(wires, x_table, spectrum):
    spaces, groups, rows, _ = wires[0].shape
    part = rows // 8

    def one_group(group, carry):
        blocks = []
        for k in range(GROUP):
            pieces = []
            for r in range(2):
                for wire in wires:
                    for source in range(spaces):
                        pieces.append(wire[source, group, pl.ds(r * GROUP + k, part, stride=8), :])
            blocks.append(dot_halves(x_table[...], jnp.concatenate(pieces, axis=0)))
        for c, block in enumerate(lane_swap(blocks)):
            spectrum[group * GROUP + c] = block.astype(BF16).astype(F32)
        return carry

    lax.fori_loop(0, groups, one_group, 0)


def scatter_modes(mixed, x_table, wires):
    spaces, _, rows, _ = wires[0].shape
    part = rows // 8
    for k, block in enumerate(lane_swap([mixed[c] for c in range(GROUP)])):
        result = dot_halves(x_table[...], block)
        place = 0
        for s in range(2):
            for wire in wires:
                for target in range(spaces):
                    wire[target, 0, pl.ds(s * GROUP + k, part, stride=8), :] = result[
                        place : place + part
                    ]
                    place += part


def mix_kernel(*refs):
    wires = refs[:CHUNKS]
    weight, x_down, x_up = refs[CHUNKS : CHUNKS + 3]
    outs = refs[CHUNKS + 3 : 2 * CHUNKS + 3]
    kept, spectrum, mixed = refs[2 * CHUNKS + 3 :]
    step = pl.program_id(0)
    channels = spectrum.shape[0]
    half = spectrum.shape[1] // 2

    @pl.when(step == 0)
    def _():
        gather_modes(wires, x_down, spectrum)
        kept[...] = spectrum[...].astype(BF16)

    real = jnp.zeros((half, 128), F32)
    imag = jnp.zeros((half, 128), F32)
    for i in range(channels):
        u_real, u_imag = spectrum[i, :half], spectrum[i, half:]
        w_real, w_imag = weight[0, i, 0].astype(F32), weight[1, i, 0].astype(F32)
        real += u_real * w_real - u_imag * w_imag
        imag += u_real * w_imag + u_imag * w_real
    place = lax.rem(step, GROUP)
    mixed[place, :half] = real
    mixed[place, half:] = imag

    @pl.when(place == GROUP - 1)
    def _():
        scatter_modes(mixed, x_up, outs)


def dual_kernel(*refs):
    wires = refs[:CHUNKS]
    weight, kept, x_down, x_up, sums = refs[CHUNKS : CHUNKS + 5]
    outs = refs[CHUNKS + 5 : 2 * CHUNKS + 5]
    slope, spectrum, mixed = refs[2 * CHUNKS + 5 :]
    step = pl.program_id(0)
    channels = spectrum.shape[0]
    half = spectrum.shape[1] // 2

    @pl.when(step == 0)
    def _():
        gather_modes(wires, x_down, spectrum)

    u_real, u_imag = kept[0, :half].astype(F32), kept[0, half:].astype(F32)
    real = jnp.zeros((half, 128), F32)
    imag = jnp.zeros((half, 128), F32)
    for o in range(channels):
        g_real, g_imag = spectrum[o, :half], spectrum[o, half:]
        w_real, w_imag = weight[0, 0, o].astype(F32), weight[1, 0, o].astype(F32)
        real += w_real * g_real + w_imag * g_imag
        imag += w_real * g_imag - w_imag * g_real
        slope[0, 0, o] = u_real * g_real + u_imag * g_imag
        slope[1, 0, o] = u_real * g_imag - u_imag * g_real
    place = lax.rem(step, GROUP)
    mixed[place, :half] = real
    mixed[place, half:] = imag

    @pl.when(place == GROUP - 1)
    def _():
        scatter_modes(mixed, x_up, outs)
        targets, _, rows, lanes = outs[-1].shape
        outs[-1][:, 0, rows - 8 :, :] = jnp.broadcast_to(sums[0][None], (targets, 8, lanes))


def mix_call(wires, weight, kept, sums, x_down, x_up):
    _, channels, _, modes_x, modes = weight.shape
    shape = wires[0].shape
    wire_block = (shape[0], 1) + shape[2:]
    wire_specs = [fixed(shape) for _ in wires]
    tables = [fixed(x_down.shape), fixed(x_up.shape)]
    out_wires = [pl.BlockSpec(wire_block, lambda s: (0, s // GROUP, 0, 0)) for _ in wires]
    out_shapes = [jax.ShapeDtypeStruct(shape, F32) for _ in wires]
    scratch = [
        pltpu.VMEM((channels, 2 * modes_x, modes), F32),
        pltpu.VMEM((GROUP, 2 * modes_x, modes), F32),
    ]
    if kept is None:
        block = (2, channels, 1, modes_x, modes)
        return pl.pallas_call(
            mix_kernel,
            grid=(channels,),
            in_specs=wire_specs + [pl.BlockSpec(block, lambda s: (0, 0, s, 0, 0))] + tables,
            out_specs=out_wires + [fixed((channels, 2 * modes_x, modes))],
            out_shape=out_shapes + [jax.ShapeDtypeStruct((channels, 2 * modes_x, modes), BF16)],
            scratch_shapes=scratch,
            compiler_params=params(),
            name="mix",
        )(*wires, weight, x_down, x_up)
    block = (2, 1, channels, modes_x, modes)
    longer = shape[2] + 8
    last_block = (shape[0], 1, longer, shape[3])
    out_wires[-1] = pl.BlockSpec(last_block, lambda s: (0, s // GROUP, 0, 0))
    out_shapes[-1] = jax.ShapeDtypeStruct(shape[:2] + (longer, shape[3]), F32)
    return pl.pallas_call(
        dual_kernel,
        grid=(channels,),
        in_specs=wire_specs
        + [
            pl.BlockSpec(block, lambda s: (0, s, 0, 0, 0)),
            pl.BlockSpec((1, 2 * modes_x, modes), lambda s: (s, 0, 0)),
        ]
        + tables
        + [pl.BlockSpec((1, 8, 128), lambda s: (s // GROUP, 0, 0))],
        out_specs=out_wires + [pl.BlockSpec(block, lambda s: (0, s, 0, 0, 0))],
        out_shape=out_shapes
        + [jax.ShapeDtypeStruct((2, channels, channels, modes_x, modes), F32)],
        scratch_shapes=scratch,
        compiler_params=params(),
        name="dual",
    )(*wires, weight, kept, x_down, x_up, sums)


def restore_planes(wire, y_table, z_table, spectral):
    spaces, groups = wire.shape[:2]
    cells_y = spectral.shape[1]
    for g in range(groups):
        coded = wire[:, g].reshape(spaces * 8, 128).astype(BF16)
        lines = dot(y_table[...], coded).astype(BF16)
        lines = jnp.concatenate([lines[:cells_y], lines[cells_y:]], axis=1)
        planes = dot(lines, z_table[...])
        for c in range(GROUP):
            spectral[g * GROUP + c] = planes[:, c * 128 : (c + 1) * 128]


def synthesise_kernel(
    wire, field, cotangent, point, bias, y_up, z_up, z_down, y_down, *refs
):
    activation, grad, wire_out, point_sum, bias_sum, spectral = refs[-6:]
    step = pl.program_id(0)
    channels, _, cells_y, cells_z = field.shape

    @pl.when(step == 0)
    def _():
        point_sum[...] = jnp.zeros_like(point_sum)
        bias_sum[...] = jnp.zeros_like(bias_sum)

    restore_planes(wire, y_up, z_up, spectral)
    for row in range(cells_y // ROWS):
        lines = pl.ds(row * ROWS, ROWS)
        inputs = field[:, 0, lines, :].reshape(channels * ROWS, cells_z)
        preact = dot(point[...], inputs)
        preact += spectral[:, lines, :].reshape(channels * ROWS, cells_z) + bias[...]
        square = preact * preact
        tangent = jnp.tanh(preact * (GELU_SCALE + (GELU_SCALE * GELU_CUBE) * square))
        upper = 0.5 + 0.5 * tangent
        activation[:, 0, lines, :] = (
            (preact * upper).astype(BF16).reshape(channels, ROWS, cells_z)
        )
        inner = GELU_SCALE + (3.0 * GELU_SCALE * GELU_CUBE) * square
        slope = upper + (preact * inner) * (0.5 - 0.5 * tangent * tangent)
        coming = cotangent[:, 0, lines, :].reshape(channels * ROWS, cells_z).astype(F32)
        low = (coming * slope).astype(BF16)
        grad[:, 0, lines, :] = low.reshape(channels, ROWS, cells_z)
        bias_sum[...] += low.astype(F32)

    def by_rows(ref):
        return jnp.concatenate(
            [
                ref[:, 0, row * ROWS : (row + 1) * ROWS, :].reshape(channels * ROWS, cells_z)
                for row in range(cells_y // ROWS)
            ],
            axis=1,
        )

    point_sum[...] += lax.dot_general(
        by_rows(field), by_rows(grad), (((1,), (1,)), ((), ())), preferred_element_type=F32
    )
    for g in range(channels // GROUP):
        planes = [grad[g * GROUP + c, 0] for c in range(GROUP)]
        coded = analyse_planes(planes, z_down[...], y_down[...])
        wire_out[:, g] = coded.reshape(wire_out.shape[0], 8, 128)


def synthesise_call(wire, field, cotangent, point, bias, tables, chunk, earlier):
    channels, planes, cells_y, cells_z = field.shape
    part = planes // CHUNKS
    spaces, groups = wire.shape[:2]
    slab = pl.BlockSpec((channels, 1, cells_y, cells_z), lambda x: (0, chunk * part + x, 0, 0))
    wire_spec = pl.BlockSpec((spaces, groups, 8, 128), lambda x: (0, 0, x, 0))
    side = channels * ROWS
    operands = [wire, field, cotangent, point, bias] + list(tables)
    specs = [wire_spec, slab, slab] + [fixed(a.shape) for a in operands[3:]]
    aliases = {}
    for index, value in enumerate(earlier):
        aliases[len(operands)] = index
        operands.append(value)
        specs.append(pl.BlockSpec(memory_space=pl.ANY))
    return pl.pallas_call(
        synthesise_kernel,
        grid=(part,),
        in_specs=specs,
        out_specs=[slab, slab, wire_spec, fixed((side, side)), fixed((side, cells_z))],
        out_shape=[
            jax.ShapeDtypeStruct(field.shape, BF16),
            jax.ShapeDtypeStruct(field.shape, BF16),
            jax.ShapeDtypeStruct(wire.shape, F32),
            jax.ShapeDtypeStruct((side, side), F32),
            jax.ShapeDtypeStruct((side, cells_z), F32),
        ],
        scratch_shapes=[pltpu.VMEM((channels, cells_y, cells_z), F32)],
        input_output_aliases=aliases,
        compiler_params=params(),
        name="synthesise",
    )(*operands)


def finish_kernel(wire, grad, point, y_up, z_up, *refs):
    grad_field, spectral = refs[-2:]
    channels, _, cells_y, cells_z = grad.shape
    restore_planes(wire, y_up, z_up, spectral)
    for row in range(cells_y // ROWS):
        lines = pl.ds(row * ROWS, ROWS)
        inputs = grad[:, 0, lines, :].reshape(channels * ROWS, cells_z)
        total = dot(point[...], inputs) + spectral[:, lines, :].reshape(channels * ROWS, cells_z)
        grad_field[:, 0, lines, :] = total.astype(BF16).reshape(channels, ROWS, cells_z)


def finish_call(wire, grad, point, y_up, z_up, chunk, earlier):
    channels, planes, cells_y, cells_z = grad.shape
    part = planes // CHUNKS
    spaces, groups = wire.shape[:2]
    slab = pl.BlockSpec((channels, 1, cells_y, cells_z), lambda x: (0, chunk * part + x, 0, 0))
    operands = [wire, grad, point, y_up, z_up]
    specs = [pl.BlockSpec((spaces, groups, 8, 128), lambda x: (0, 0, x, 0)), slab]
    specs += [fixed(a.shape) for a in operands[2:]]
    aliases = {}
    for value in earlier:
        aliases[len(operands)] = 0
        operands.append(value)
        specs.append(pl.BlockSpec(memory_space=pl.ANY))
    return pl.pallas_call(
        finish_kernel,
        grid=(part,),
        in_specs=specs,
        out_specs=slab,
        out_shape=jax.ShapeDtypeStruct(grad.shape, BF16),
        scratch_shapes=[pltpu.VMEM((channels, cells_y, cells_z), F32)],
        input_output_aliases=aliases,
        compiler_params=params(),
        name="finish",
    )(*operands)


def exchange(values):
    return lax.all_to_all(values, "space", split_axis=0, concat_axis=0, tiled=True)


def blocked_body(field, cotangent, spectral_weight, point_weight, bias):
    spaces = lax.axis_size("space")
    _, channels, planes, cells_y, cells_z = field.shape
    cells_x = planes * spaces
    tables = blocked_tables(cells_x, cells_y, cells_z, spaces, CHUNKS)
    z_down, z_down2, z_up, z_up2, y_down, y_up, x_down, x_up = map(jnp.asarray, tables)
    field_part, cotangent_part = field[0], cotangent[0]
    eye = jnp.eye(ROWS, dtype=F32)
    point_in = jnp.kron(point_weight.T.astype(F32), eye).astype(BF16)
    point_out = jnp.kron(point_weight.astype(F32), eye).astype(BF16)
    bias_rows = jnp.broadcast_to(jnp.repeat(bias, ROWS)[:, None], (channels * ROWS, cells_z))
    chunks = range(CHUNKS)
    wires = [exchange(analyse_call(field_part, z_down, y_down, spaces, h)) for h in chunks]
    *wires, kept = mix_call(wires, spectral_weight, None, None, x_down, x_up)
    wires = [exchange(w) for w in wires]
    earlier, back, point_sums, bias_sums = [], [], 0.0, 0.0
    for h in chunks:
        activation, grad, wire, point_sum, bias_sum = synthesise_call(
            wires[h], field_part, cotangent_part, point_in, bias_rows,
            (y_up, z_up2, z_down2, y_down), h, earlier,
        )
        earlier = [activation, grad]
        back.append(exchange(wire))
        point_sums, bias_sums = point_sums + point_sum, bias_sums + bias_sum
    point_part = jnp.sum(
        point_sums.reshape(channels, ROWS, channels, ROWS) * eye[None, :, None, :], axis=(1, 3)
    )
    bias_part = jnp.sum(bias_sums.reshape(channels, -1), axis=1)
    sums = jnp.concatenate([point_part.reshape(-1), bias_part])
    groups = channels // GROUP
    padded = jnp.pad(sums, (0, groups * 1024 - sums.shape[0])).reshape(groups, 8, 128)
    *wires, grad_spectral = mix_call(back, spectral_weight, kept, padded, x_down, x_up)
    wires = [exchange(w) for w in wires]
    totals = jnp.sum(wires[-1][:, :, -8:, :], axis=0).reshape(-1)
    point_total = totals[: channels * channels].reshape(channels, channels)
    bias_total = totals[channels * channels : channels * (channels + 1)]
    finished = []
    for h in chunks:
        finished = [finish_call(wires[h], grad, point_out, y_up, z_up, h, finished)]
    factor = 1.0 / math.sqrt(cells_x * cells_y * cells_z)
    return (
        activation[None],
        finished[0][None],
        grad_spectral,
        point_total * factor,
        bias_total * factor,
    )


def body(field, cotangent, spectral_weight, point_weight, bias):
    blocked = (
        field.shape == (1, 16, 16, 256, 128)
        and spectral_weight.shape == (2, 16, 16, 64, 128)
        and lax.axis_size("space") == 16
    )
    chosen = blocked_body if blocked else general_body
    return chosen(field, cotangent, spectral_weight, point_weight, bias)


def solution(mesh):
    placed = (
        P("groups", None, "space", None, None),
        P("groups", None, "space", None, None),
        P(None, None, None, None, "space"),
        P(),
        P(),
    )
    return jax.shard_map(
        body,
        mesh=mesh,
        in_specs=placed,
        out_specs=(
            P("groups", None, "space", None, None),
            P("groups", None, "space", None, None),
            P("groups", None, None, None, "space"),
            P("groups", None),
            P("groups"),
        ),
        check_vma=False,
    )
```

```python
import math

import jax
import numpy as np
import jax.numpy as jnp
from jax import lax
from jax.experimental import pallas as pl
from jax.experimental.pallas import tpu as pltpu
from jax.sharding import PartitionSpec as P

MODES = 32


TURN = 2.0 * math.pi
GELU_SCALE = math.sqrt(2.0 / math.pi)
GELU_CUBE = 0.044715
PRECISE = lax.Precision.HIGHEST


def twiddle(length, frequencies):
    places = jnp.arange(length, dtype=jnp.int32)[:, None]
    phase = (places * frequencies[None, :] % length).astype(jnp.float32) * (TURN / length)
    factor = 1.0 / math.sqrt(length)
    return (jnp.cos(phase) * factor, -jnp.sin(phase) * factor)


def kept_modes(length, modes):
    return jnp.concatenate(
        [jnp.arange(modes, dtype=jnp.int32), jnp.arange(length - modes, length, dtype=jnp.int32)]
    )


def block_table(real_part, imag_part):
    upper = jnp.stack([real_part, imag_part], axis=1)
    lower = jnp.stack([-imag_part, real_part], axis=1)
    return jnp.stack([upper, lower], axis=1)


def make_tables(cells_x, cells_y, cells_z, modes):
    z_real, z_imag = twiddle(cells_z, jnp.arange(modes, dtype=jnp.int32))
    forward_z = jnp.concatenate([z_real, z_imag], axis=1)
    doubling = jnp.where(jnp.arange(modes, dtype=jnp.int32) == 0, 1.0, 2.0).astype(jnp.float32)
    double_z = forward_z * jnp.concatenate([doubling, doubling])[None, :]
    y_real, y_imag = twiddle(cells_y, kept_modes(cells_y, modes))
    full_y = block_table(y_real, y_imag)
    x_real, x_imag = twiddle(cells_x, kept_modes(cells_x, modes))
    full_x = block_table(x_real, x_imag)
    return (
        forward_z.astype(jnp.bfloat16),
        double_z.astype(jnp.bfloat16),
        full_y.astype(jnp.bfloat16),
        full_y,
        full_x,
    )


def analyse_slab(values, z_table, y_table):
    zspec = jnp.dot(values, z_table, preferred_element_type=jnp.float32).astype(jnp.bfloat16)
    shape = zspec.shape
    split_values = zspec.reshape(shape[:4] + (2, shape[4] // 2))
    result = jnp.einsum(
        "bcxyrk,yrsq->bcxsqk", split_values, y_table, preferred_element_type=jnp.float32
    )
    rshape = result.shape
    return result.reshape(rshape[:4] + (rshape[4] * rshape[5],))


def restore_slab(values, y_table, z_table):
    shape = values.shape
    modes_y = y_table.shape[3]
    split_values = values.reshape(shape[:4] + (modes_y, shape[4] // modes_y))
    result = jnp.einsum("bcxrqk,ysrq->bcxysk", split_values, y_table, precision=PRECISE)
    rshape = result.shape
    rounded = result.reshape(rshape[:4] + (rshape[4] * rshape[5],)).astype(jnp.bfloat16)
    return jnp.dot(rounded, z_table.T, preferred_element_type=jnp.float32)


def x_forward(values, table):
    return jnp.einsum("bcxrm,xrsq->bcsqm", values, table, precision=PRECISE)


def x_inverse(values, table):
    return jnp.einsum("bcrqm,xsrq->bcxsm", values, table, precision=PRECISE)


def gelu_parts(preact):
    cube = preact * preact * preact
    tangent = jnp.tanh(GELU_SCALE * (preact + GELU_CUBE * cube))
    value = 0.5 * preact * (1.0 + tangent)
    slope = 0.5 * (1.0 + tangent) + 0.5 * preact * (1.0 - tangent * tangent) * GELU_SCALE * (
        1.0 + 3.0 * GELU_CUBE * preact * preact
    )
    return (value, slope)


def contract(form, left, right):
    return jnp.einsum(form, left, right, preferred_element_type=jnp.float32)


def mix_forward(spectrum, weight):
    u_real, u_imag = (spectrum[:, :, 0], spectrum[:, :, 1])
    w_real, w_imag = (weight[0], weight[1])
    form = "bikm,iokm->bokm"
    out_real = contract(form, u_real, w_real) - contract(form, u_imag, w_imag)
    out_imag = contract(form, u_real, w_imag) + contract(form, u_imag, w_real)
    return jnp.stack([out_real, out_imag], axis=2)


def mix_dual(grads, weight):
    g_real, g_imag = (grads[:, :, 0], grads[:, :, 1])
    w_real, w_imag = (weight[0], weight[1])
    form = "bokm,iokm->bikm"
    in_real = contract(form, g_real, w_real) + contract(form, g_imag, w_imag)
    in_imag = contract(form, g_imag, w_real) - contract(form, g_real, w_imag)
    return jnp.stack([in_real, in_imag], axis=2)


def weight_grad(spectrum, grads):
    u_real, u_imag = (spectrum[:, :, 0], spectrum[:, :, 1])
    g_real, g_imag = (grads[:, :, 0], grads[:, :, 1])
    form = "bikm,bokm->iokm"
    part_real = contract(form, u_real, g_real) + contract(form, u_imag, g_imag)
    part_imag = contract(form, u_real, g_imag) - contract(form, u_imag, g_real)
    return jnp.stack([part_real, part_imag], axis=0)


def general_body(field, cotangent, spectral_weight, point_weight, bias):
    spaces = lax.axis_size("space")
    planes = field.shape[2]
    cells_y = field.shape[3]
    cells_z = field.shape[4]
    cells_x = planes * spaces
    forward_z, double_z, half_y, full_y, full_x = make_tables(cells_x, cells_y, cells_z, MODES)

    def x_step(values):
        return x_forward(values, full_x)

    spectrum = analyse_slab(field, forward_z, half_y)
    owned = x_step(lax.all_to_all(spectrum, "space", split_axis=4, concat_axis=2, tiled=True))
    owned_low = owned.astype(jnp.bfloat16)
    mixed = mix_forward(owned_low, spectral_weight)
    xback = x_inverse(mixed, full_x)
    returned = lax.all_to_all(xback, "space", split_axis=2, concat_axis=4, tiled=True)
    spectral_part = restore_slab(returned, full_y, double_z)
    pointwise = contract("oi,bixyz->boxyz", point_weight.T, field)
    preact = spectral_part + pointwise + bias[None, :, None, None, None]
    value, slope = gelu_parts(preact)
    activation = value.astype(jnp.bfloat16)
    grad_low = (cotangent.astype(jnp.float32) * slope).astype(jnp.bfloat16)
    point_sum = contract("bixyz,boxyz->io", field, grad_low)
    bias_sum = jnp.sum(grad_low, axis=(0, 2, 3, 4), dtype=jnp.float32)
    point_total, bias_total = lax.psum((point_sum, bias_sum), "space")
    grad_spec = analyse_slab(grad_low, double_z, half_y)
    grad_owned = x_step(lax.all_to_all(grad_spec, "space", split_axis=4, concat_axis=2, tiled=True))
    grad_owned_low = grad_owned.astype(jnp.bfloat16)
    grad_spectral = weight_grad(owned_low, grad_owned_low)
    dual = mix_dual(grad_owned_low, spectral_weight)
    dxback = x_inverse(dual, full_x)
    dreturned = lax.all_to_all(dxback, "space", split_axis=2, concat_axis=4, tiled=True)
    spectral_grad = restore_slab(dreturned, full_y, forward_z)
    total = spectral_grad + contract("io,boxyz->bixyz", point_weight, grad_low)
    grad_field = total.astype(jnp.bfloat16)
    factor = 1.0 / math.sqrt(cells_x * cells_y * cells_z)
    return (activation, grad_field, grad_spectral, point_total * factor, bias_total * factor)


CHUNKS = 2
GROUP = 4
ROWS = 16
VMEM = 56 * 1024 * 1024
BF16 = jnp.bfloat16
F32 = jnp.float32


def np_twiddle(length, frequencies):
    phase = (np.arange(length)[:, None] * frequencies[None, :] % length) * (TURN / length)
    factor = 1.0 / math.sqrt(length)
    return np.cos(phase) * factor, -np.sin(phase) * factor


def np_block(length, modes):
    kept = np.concatenate([np.arange(modes), np.arange(length - modes, length)])
    real, imag = np_twiddle(length, kept)
    return np.stack([np.stack([real, imag], 1), np.stack([-imag, real], 1)], 1)


def in_halves(table):
    high = table.astype(BF16)
    low = (table - high.astype(np.float64)).astype(BF16)
    return np.concatenate([high, high, low], axis=1)


def blocked_tables(cells_x, cells_y, cells_z, spaces, chunks):
    z_real, z_imag = np_twiddle(cells_z, np.arange(MODES))
    forward_z = np.stack([z_real, z_imag], 1)
    doubling = np.where(np.arange(MODES) == 0, 1.0, 2.0)
    double_z = forward_z * doubling
    eye = np.eye(GROUP)

    def z_down(table):
        out = np.einsum("zrk,ab->azrbk", table, eye)
        return out.reshape(GROUP * cells_z, 2 * GROUP * MODES).astype(BF16)

    full_y = np_block(cells_y, MODES)
    y_split = full_y.reshape(cells_y, 2, 2, spaces, 2 * MODES // spaces)
    y_down = y_split.transpose(3, 2, 4, 1, 0).reshape(4 * MODES, 2 * cells_y).astype(BF16)
    y_up = y_split.transpose(1, 0, 3, 2, 4).reshape(2 * cells_y, 4 * MODES).astype(BF16)
    full_x = np_block(cells_x, MODES)
    x_split = full_x.reshape(spaces, chunks, cells_x // spaces // chunks, 2, 2, 2 * MODES)
    x_split = x_split.transpose(1, 0, 2, 3, 4, 5).reshape(cells_x, 2, 2, 2 * MODES)
    x_down = x_split.transpose(2, 3, 1, 0).reshape(4 * MODES, 2 * cells_x)
    x_up = x_split.transpose(1, 0, 2, 3).reshape(2 * cells_x, 4 * MODES)
    forward, double = z_down(forward_z), z_down(double_z)
    return forward, double, forward.T.copy(), double.T.copy(), y_down, y_up, in_halves(x_down), in_halves(x_up)


def dot(left, right):
    return jnp.dot(left, right, preferred_element_type=F32)


def dot_halves(table, values):
    high = values.astype(BF16)
    low = (values - high.astype(F32)).astype(BF16)
    return dot(table, jnp.concatenate([high, low, high], axis=0))


def params():
    return pltpu.CompilerParams(vmem_limit_bytes=VMEM)


def fixed(shape):
    return pl.BlockSpec(shape, lambda *_: (0,) * len(shape))


def analyse_planes(planes, z_table, y_table):
    spectrum = dot(jnp.concatenate(planes, axis=1), z_table).astype(BF16)
    half = spectrum.shape[1] // 2
    stacked = jnp.concatenate([spectrum[:, :half], spectrum[:, half:]], axis=0)
    return dot(y_table, stacked)


def analyse_kernel(field, z_table, y_table, wire):
    count = field.shape[1]
    for place in range(count):
        planes = [field[c, place] for c in range(GROUP)]
        coded = analyse_planes(planes, z_table[...], y_table[...])
        wire[:, 0, place * 8 : place * 8 + 8, :] = coded.reshape(wire.shape[0], 8, 128)


def analyse_call(field, z_table, y_table, spaces, chunk):
    channels, planes, cells_y, cells_z = field.shape
    part = planes
    step = min(4, part)
    return pl.pallas_call(
        analyse_kernel,
        grid=(channels // GROUP, part // step),
        in_specs=[
            pl.BlockSpec(
                (GROUP, step, cells_y, cells_z),
                lambda g, x: (g, chunk * (part // step) + x, 0, 0),
            ),
            fixed(z_table.shape),
            fixed(y_table.shape),
        ],
        out_specs=pl.BlockSpec((spaces, 1, step * 8, 128), lambda g, x: (0, g, x, 0)),
        out_shape=jax.ShapeDtypeStruct((spaces, channels // GROUP, part * 8, 128), F32),
        compiler_params=params(),
        name="analyse",
    )(field, z_table, y_table)


def lane_swap(blocks):
    return [
        jnp.concatenate([b[:, k * MODES : (k + 1) * MODES] for b in blocks], axis=1)
        for k in range(GROUP)
    ]


def gather_modes(wires, x_table, spectrum):
    spaces, groups, rows, _ = wires[0].shape
    part = rows // 8

    def one_group(group, carry):
        blocks = []
        for k in range(GROUP):
            pieces = []
            for r in range(2):
                for wire in wires:
                    for source in range(spaces):
                        pieces.append(wire[source, group, pl.ds(r * GROUP + k, part, stride=8), :])
            blocks.append(dot_halves(x_table[...], jnp.concatenate(pieces, axis=0)))
        for c, block in enumerate(lane_swap(blocks)):
            spectrum[group * GROUP + c] = block.astype(BF16).astype(F32)
        return carry

    lax.fori_loop(0, groups, one_group, 0)


def scatter_modes(mixed, x_table, wires):
    spaces, _, rows, _ = wires[0].shape
    part = rows // 8
    for k, block in enumerate(lane_swap([mixed[c] for c in range(GROUP)])):
        result = dot_halves(x_table[...], block)
        place = 0
        for s in range(2):
            for wire in wires:
                for target in range(spaces):
                    wire[target, 0, pl.ds(s * GROUP + k, part, stride=8), :] = result[
                        place : place + part
                    ]
                    place += part


def mix_kernel(*refs):
    wires = refs[:1]
    weight, x_down, x_up = refs[1:4]
    outs = refs[4 : CHUNKS + 4]
    kept, spectrum, mixed = refs[CHUNKS + 4 :]
    step = pl.program_id(0)
    channels = spectrum.shape[0]
    half = spectrum.shape[1] // 2

    @pl.when(step == 0)
    def _():
        gather_modes(wires, x_down, spectrum)
        kept[...] = spectrum[...].astype(BF16)

    real = jnp.zeros((half, 128), F32)
    imag = jnp.zeros((half, 128), F32)
    for i in range(channels):
        u_real, u_imag = spectrum[i, :half], spectrum[i, half:]
        w_real, w_imag = weight[0, i, 0].astype(F32), weight[1, i, 0].astype(F32)
        real += u_real * w_real - u_imag * w_imag
        imag += u_real * w_imag + u_imag * w_real
    place = lax.rem(step, GROUP)
    mixed[place, :half] = real
    mixed[place, half:] = imag

    @pl.when(place == GROUP - 1)
    def _():
        scatter_modes(mixed, x_up, outs)


def dual_kernel(*refs):
    wires = refs[:CHUNKS]
    weight, kept, x_down, x_up, sums = refs[CHUNKS : CHUNKS + 5]
    outs = refs[CHUNKS + 5 : 2 * CHUNKS + 5]
    slope, spectrum, mixed = refs[2 * CHUNKS + 5 :]
    step = pl.program_id(0)
    channels = spectrum.shape[0]
    half = spectrum.shape[1] // 2

    @pl.when(step == 0)
    def _():
        gather_modes(wires, x_down, spectrum)

    u_real, u_imag = kept[0, :half].astype(F32), kept[0, half:].astype(F32)
    real = jnp.zeros((half, 128), F32)
    imag = jnp.zeros((half, 128), F32)
    for o in range(channels):
        g_real, g_imag = spectrum[o, :half], spectrum[o, half:]
        w_real, w_imag = weight[0, 0, o].astype(F32), weight[1, 0, o].astype(F32)
        real += w_real * g_real + w_imag * g_imag
        imag += w_real * g_imag - w_imag * g_real
        slope[0, 0, o] = u_real * g_real + u_imag * g_imag
        slope[1, 0, o] = u_real * g_imag - u_imag * g_real
    place = lax.rem(step, GROUP)
    mixed[place, :half] = real
    mixed[place, half:] = imag

    @pl.when(place == GROUP - 1)
    def _():
        scatter_modes(mixed, x_up, outs)
        targets, _, rows, lanes = outs[-1].shape
        outs[-1][:, 0, rows - 8 :, :] = jnp.broadcast_to(sums[0][None], (targets, 8, lanes))


def mix_call(wires, weight, kept, sums, x_down, x_up):
    _, channels, _, modes_x, modes = weight.shape
    wire_specs = [fixed(wire.shape) for wire in wires]
    shape = wires[0].shape
    shape = shape[:2] + (shape[2] * len(wires) // CHUNKS, shape[3])
    wire_block = (shape[0], 1) + shape[2:]
    tables = [fixed(x_down.shape), fixed(x_up.shape)]
    out_wires = [pl.BlockSpec(wire_block, lambda s: (0, s // GROUP, 0, 0)) for _ in range(CHUNKS)]
    out_shapes = [jax.ShapeDtypeStruct(shape, F32) for _ in range(CHUNKS)]
    scratch = [
        pltpu.VMEM((channels, 2 * modes_x, modes), F32),
        pltpu.VMEM((GROUP, 2 * modes_x, modes), F32),
    ]
    if kept is None:
        block = (2, channels, 1, modes_x, modes)
        return pl.pallas_call(
            mix_kernel,
            grid=(channels,),
            in_specs=wire_specs + [pl.BlockSpec(block, lambda s: (0, 0, s, 0, 0))] + tables,
            out_specs=out_wires + [fixed((channels, 2 * modes_x, modes))],
            out_shape=out_shapes + [jax.ShapeDtypeStruct((channels, 2 * modes_x, modes), BF16)],
            scratch_shapes=scratch,
            compiler_params=params(),
            name="mix",
        )(*wires, weight, x_down, x_up)
    block = (2, 1, channels, modes_x, modes)
    longer = shape[2] + 8
    last_block = (shape[0], 1, longer, shape[3])
    out_wires[-1] = pl.BlockSpec(last_block, lambda s: (0, s // GROUP, 0, 0))
    out_shapes[-1] = jax.ShapeDtypeStruct(shape[:2] + (longer, shape[3]), F32)
    return pl.pallas_call(
        dual_kernel,
        grid=(channels,),
        in_specs=wire_specs
        + [
            pl.BlockSpec(block, lambda s: (0, s, 0, 0, 0)),
            pl.BlockSpec((1, 2 * modes_x, modes), lambda s: (s, 0, 0)),
        ]
        + tables
        + [pl.BlockSpec((1, 8, 128), lambda s: (s // GROUP, 0, 0))],
        out_specs=out_wires + [pl.BlockSpec(block, lambda s: (0, s, 0, 0, 0))],
        out_shape=out_shapes
        + [jax.ShapeDtypeStruct((2, channels, channels, modes_x, modes), F32)],
        scratch_shapes=scratch,
        compiler_params=params(),
        name="dual",
    )(*wires, weight, kept, x_down, x_up, sums)


def restore_planes(wire, y_table, z_table, spectral):
    spaces, groups = wire.shape[:2]
    cells_y = spectral.shape[1]
    for g in range(groups):
        coded = wire[:, g].reshape(spaces * 8, 128).astype(BF16)
        lines = dot(y_table[...], coded).astype(BF16)
        lines = jnp.concatenate([lines[:cells_y], lines[cells_y:]], axis=1)
        planes = dot(lines, z_table[...])
        for c in range(GROUP):
            spectral[g * GROUP + c] = planes[:, c * 128 : (c + 1) * 128]


def synthesise_kernel(
    wire, field, cotangent, point, bias, y_up, z_up, z_down, y_down, *refs
):
    activation, grad, wire_out, point_sum, bias_sum, spectral = refs[-6:]
    step = pl.program_id(0)
    channels, _, cells_y, cells_z = field.shape

    @pl.when(step == 0)
    def _():
        point_sum[...] = jnp.zeros_like(point_sum)
        bias_sum[...] = jnp.zeros_like(bias_sum)

    restore_planes(wire, y_up, z_up, spectral)
    for row in range(cells_y // ROWS):
        lines = pl.ds(row * ROWS, ROWS)
        inputs = field[:, 0, lines, :].reshape(channels * ROWS, cells_z)
        preact = dot(point[...], inputs)
        preact += spectral[:, lines, :].reshape(channels * ROWS, cells_z) + bias[...]
        square = preact * preact
        tangent = jnp.tanh(preact * (GELU_SCALE + (GELU_SCALE * GELU_CUBE) * square))
        upper = 0.5 + 0.5 * tangent
        activation[:, 0, lines, :] = (
            (preact * upper).astype(BF16).reshape(channels, ROWS, cells_z)
        )
        inner = GELU_SCALE + (3.0 * GELU_SCALE * GELU_CUBE) * square
        slope = upper + (preact * inner) * (0.5 - 0.5 * tangent * tangent)
        coming = cotangent[:, 0, lines, :].reshape(channels * ROWS, cells_z).astype(F32)
        low = (coming * slope).astype(BF16)
        grad[:, 0, lines, :] = low.reshape(channels, ROWS, cells_z)
        bias_sum[...] += low.astype(F32)

    def by_rows(ref):
        return jnp.concatenate(
            [
                ref[:, 0, row * ROWS : (row + 1) * ROWS, :].reshape(channels * ROWS, cells_z)
                for row in range(cells_y // ROWS)
            ],
            axis=1,
        )

    point_sum[...] += lax.dot_general(
        by_rows(field), by_rows(grad), (((1,), (1,)), ((), ())), preferred_element_type=F32
    )
    for g in range(channels // GROUP):
        planes = [grad[g * GROUP + c, 0] for c in range(GROUP)]
        coded = analyse_planes(planes, z_down[...], y_down[...])
        wire_out[:, g] = coded.reshape(wire_out.shape[0], 8, 128)


def synthesise_call(wire, field, cotangent, point, bias, tables, chunk, earlier):
    channels, planes, cells_y, cells_z = field.shape
    part = planes // CHUNKS
    spaces, groups = wire.shape[:2]
    slab = pl.BlockSpec((channels, 1, cells_y, cells_z), lambda x: (0, chunk * part + x, 0, 0))
    wire_spec = pl.BlockSpec((spaces, groups, 8, 128), lambda x: (0, 0, x, 0))
    side = channels * ROWS
    operands = [wire, field, cotangent, point, bias] + list(tables)
    specs = [wire_spec, slab, slab] + [fixed(a.shape) for a in operands[3:]]
    aliases = {}
    for index, value in enumerate(earlier):
        aliases[len(operands)] = index
        operands.append(value)
        specs.append(pl.BlockSpec(memory_space=pl.ANY))
    return pl.pallas_call(
        synthesise_kernel,
        grid=(part,),
        in_specs=specs,
        out_specs=[slab, slab, wire_spec, fixed((side, side)), fixed((side, cells_z))],
        out_shape=[
            jax.ShapeDtypeStruct(field.shape, BF16),
            jax.ShapeDtypeStruct(field.shape, BF16),
            jax.ShapeDtypeStruct(wire.shape, F32),
            jax.ShapeDtypeStruct((side, side), F32),
            jax.ShapeDtypeStruct((side, cells_z), F32),
        ],
        scratch_shapes=[pltpu.VMEM((channels, cells_y, cells_z), F32)],
        input_output_aliases=aliases,
        compiler_params=params(),
        name="synthesise",
    )(*operands)


def finish_kernel(wire, grad, point, y_up, z_up, *refs):
    grad_field, spectral = refs[-2:]
    channels, _, cells_y, cells_z = grad.shape
    restore_planes(wire, y_up, z_up, spectral)
    for row in range(cells_y // ROWS):
        lines = pl.ds(row * ROWS, ROWS)
        inputs = grad[:, 0, lines, :].reshape(channels * ROWS, cells_z)
        total = dot(point[...], inputs) + spectral[:, lines, :].reshape(channels * ROWS, cells_z)
        grad_field[:, 0, lines, :] = total.astype(BF16).reshape(channels, ROWS, cells_z)


def finish_call(wire, grad, point, y_up, z_up, chunk, earlier):
    channels, planes, cells_y, cells_z = grad.shape
    part = planes // CHUNKS
    spaces, groups = wire.shape[:2]
    slab = pl.BlockSpec((channels, 1, cells_y, cells_z), lambda x: (0, chunk * part + x, 0, 0))
    operands = [wire, grad, point, y_up, z_up]
    specs = [pl.BlockSpec((spaces, groups, 8, 128), lambda x: (0, 0, x, 0)), slab]
    specs += [fixed(a.shape) for a in operands[2:]]
    aliases = {}
    for value in earlier:
        aliases[len(operands)] = 0
        operands.append(value)
        specs.append(pl.BlockSpec(memory_space=pl.ANY))
    return pl.pallas_call(
        finish_kernel,
        grid=(part,),
        in_specs=specs,
        out_specs=slab,
        out_shape=jax.ShapeDtypeStruct(grad.shape, BF16),
        scratch_shapes=[pltpu.VMEM((channels, cells_y, cells_z), F32)],
        input_output_aliases=aliases,
        compiler_params=params(),
        name="finish",
    )(*operands)


def exchange(values):
    return lax.all_to_all(values, "space", split_axis=0, concat_axis=0, tiled=True)


def blocked_body(field, cotangent, spectral_weight, point_weight, bias):
    spaces = lax.axis_size("space")
    _, channels, planes, cells_y, cells_z = field.shape
    cells_x = planes * spaces
    tables = blocked_tables(cells_x, cells_y, cells_z, spaces, CHUNKS)
    z_down, z_down2, z_up, z_up2, y_down, y_up, x_down, x_up = map(jnp.asarray, tables)
    field_part, cotangent_part = field[0], cotangent[0]
    eye = jnp.eye(ROWS, dtype=F32)
    point_in = jnp.kron(point_weight.T.astype(F32), eye).astype(BF16)
    point_out = jnp.kron(point_weight.astype(F32), eye).astype(BF16)
    bias_rows = jnp.broadcast_to(jnp.repeat(bias, ROWS)[:, None], (channels * ROWS, cells_z))
    chunks = range(CHUNKS)
    wires = [exchange(analyse_call(field_part, z_down, y_down, spaces, 0))]
    x_whole = jnp.asarray(blocked_tables(cells_x, cells_y, cells_z, spaces, 1)[6])
    *wires, kept = mix_call(wires, spectral_weight, None, None, x_whole, x_up)
    wires = [exchange(w) for w in wires]
    earlier, back, point_sums, bias_sums = [], [], 0.0, 0.0
    for h in chunks:
        activation, grad, wire, point_sum, bias_sum = synthesise_call(
            wires[h], field_part, cotangent_part, point_in, bias_rows,
            (y_up, z_up2, z_down2, y_down), h, earlier,
        )
        earlier = [activation, grad]
        back.append(exchange(wire))
        point_sums, bias_sums = point_sums + point_sum, bias_sums + bias_sum
    point_part = jnp.sum(
        point_sums.reshape(channels, ROWS, channels, ROWS) * eye[None, :, None, :], axis=(1, 3)
    )
    bias_part = jnp.sum(bias_sums.reshape(channels, -1), axis=1)
    sums = jnp.concatenate([point_part.reshape(-1), bias_part])
    groups = channels // GROUP
    padded = jnp.pad(sums, (0, groups * 1024 - sums.shape[0])).reshape(groups, 8, 128)
    *wires, grad_spectral = mix_call(back, spectral_weight, kept, padded, x_down, x_up)
    wires = [exchange(w) for w in wires]
    totals = jnp.sum(wires[-1][:, :, -8:, :], axis=0).reshape(-1)
    point_total = totals[: channels * channels].reshape(channels, channels)
    bias_total = totals[channels * channels : channels * (channels + 1)]
    finished = []
    for h in chunks:
        finished = [finish_call(wires[h], grad, point_out, y_up, z_up, h, finished)]
    factor = 1.0 / math.sqrt(cells_x * cells_y * cells_z)
    return (
        activation[None],
        finished[0][None],
        grad_spectral,
        point_total * factor,
        bias_total * factor,
    )


def body(field, cotangent, spectral_weight, point_weight, bias):
    blocked = (
        field.shape == (1, 16, 16, 256, 128)
        and spectral_weight.shape == (2, 16, 16, 64, 128)
        and lax.axis_size("space") == 16
    )
    chosen = blocked_body if blocked else general_body
    return chosen(field, cotangent, spectral_weight, point_weight, bias)


def solution(mesh):
    placed = (
        P("groups", None, "space", None, None),
        P("groups", None, "space", None, None),
        P(None, None, None, None, "space"),
        P(),
        P(),
    )
    return jax.shard_map(
        body,
        mesh=mesh,
        in_specs=placed,
        out_specs=(
            P("groups", None, "space", None, None),
            P("groups", None, "space", None, None),
            P("groups", None, None, None, "space"),
            P("groups", None),
            P("groups"),
        ),
        check_vma=False,
    )
```
